32 devices in a mesh: section: 4 (over z), sector: 4 (over y, core), comp: 2 (over x).
Axes of the slice: x: 2, y: 2, z: 4, core: 2. Of those that a mesh axis runs over, the one named last changes fastest.
Arguments:
- env_in: bfloat16 [2, 8, 4, 512, 128], P('comp', None, 'sector', 'section'), may hold values from -6 to 6
- site_tensor: bfloat16 [3, 4, 512, 4, 512], P(None, 'sector', None, None, 'section'), may hold values from -0.125 to 0.125
- bra_tensor: bfloat16 [3, 4, 128, 4, 128], P(None, 'sector'), may hold values from -0.5 to 0.5
- mixing: float32 [3, 4, 8, 8], replicated, may hold values from -2 to 2
- sector_sizes: int32 [4, 4], replicated, may hold values from 256 to 512, as said below
- targets: int32 [3, 4, 4], replicated, may hold values from 0 to 3, as said below
Outputs:
- env_out: bfloat16 [3, 2, 8, 4, 512, 128], P(None, 'comp', None, 'sector', 'section')
- total_env: bfloat16 [8, 4, 512, 128], P('comp', 'sector', 'section')
The draws below stay inside these ranges and needn't reach their ends.
Inputs may be any that keep to these rules, and one draw needn't show every extreme that they name: `sector_sizes`: on every bond some sector has exactly 512 states. For each site and source sector a the 4 targets are distinct and differ from a by at most 3; at every site some target lies 3 above its source sector and some 3 below.
All inputs are finite; a program needn't handle non-finite values.
Results may differ from the reference program's by a relative error of at most 0.02.
Values may be sent and summed in bfloat16 or wider, within the bound.
A program may use at most 64 MiB of HBM per device.

```python
import jax
import jax.numpy as jnp
from jax import lax

MAXSEC = 512
KW = 128
COMPS = 8
STATES = 4
SITES = 3
BATCHES = 2
SECTORS = 4


def draw_sector_sizes(key, part):
    drawn = jax.random.randint(key, (SITES + 1, SECTORS), MAXSEC // 2, MAXSEC + 1)
    chosen = jax.random.randint(jax.random.fold_in(key, 1), (SITES + 1, 1), 0, SECTORS)
    column = jnp.arange(SECTORS, dtype=jnp.int32)[None, :]
    return jnp.where(column == chosen, MAXSEC, drawn).astype(jnp.int32)


def draw_targets(key, part):
    span_max = STATES - 1
    width_all = 2 * span_max + 1
    deltas = jnp.arange(width_all, dtype=jnp.int32) - span_max
    source = jnp.arange(SECTORS, dtype=jnp.int32)[:, None]
    landing = source + deltas[None, :]
    allowed = jnp.logical_and(landing >= 0, landing < SECTORS)
    jitter = jax.random.randint(key, (SITES, SECTORS, width_all), 0, 1024)
    column = jnp.arange(width_all, dtype=jnp.int32)[None, None, :]
    scores = jnp.where(allowed[None, :, :], jitter * width_all + column, -1 - column)
    values, picked = lax.top_k(scores, STATES)
    order_key = jax.random.randint(jax.random.fold_in(key, 4), (SITES, SECTORS, STATES), 0, 1024) * STATES + jnp.arange(STATES, dtype=jnp.int32)[None, None, :]
    reorder = jnp.argsort(order_key, axis=-1)
    picked = jnp.take_along_axis(picked, reorder, axis=-1)
    return (source[None, :, :] + picked - span_max).astype(jnp.int32)


def steps_of(stream_key, shape, shards, low, high):
    factor_of, own = 1.0, jax.random.fold_in(stream_key, 6)
    for dim, blocks in shards:
        heights = jnp.exp(jax.random.uniform(jax.random.fold_in(own, dim), (blocks,), jnp.float32, low / len(shards), high / len(shards)))
        factor_of = factor_of * jnp.repeat(heights, shape[dim] // blocks).reshape([-1 if axis == dim else 1 for axis in range(len(shape))])
    return factor_of


def centred(stream_key, shape, scale, bound, pieces=(), kind=jnp.bfloat16):
    array = scale * jax.random.normal(stream_key, shape, jnp.float32)
    if pieces:
        array = array * steps_of(stream_key, shape, pieces, -0.22, 0.18)
    return jnp.clip(array, -bound, bound).astype(kind)


def setup_inputs(seed: int = 0) -> dict:
    splits = jax.random.split(jax.random.key(seed), 7)
    return {
        "env_in": centred(splits[0], (BATCHES, COMPS, SECTORS, MAXSEC, KW), 1.0, 6.0, ((0, 2), (2, 4), (3, 4))),
        "site_tensor": centred(splits[1], (SITES, SECTORS, MAXSEC, STATES, MAXSEC), (STATES * MAXSEC) ** -0.5, 0.125, ((1, 4), (4, 4))),
        "bra_tensor": centred(splits[2], (SITES, SECTORS, KW, STATES, KW), KW ** -0.5, 0.5, ((1, 4),)),
        "mixing": centred(splits[3], (SITES, STATES, COMPS, COMPS), COMPS ** -0.5, 2.0, (), jnp.float32),
        "sector_sizes": draw_sector_sizes(jax.random.fold_in(splits[6], 71), 0),
        "targets": draw_targets(jax.random.fold_in(splits[6], 71), 0),
    }


def reference(env_in, site_tensor, bra_tensor, mixing, sector_sizes, targets):
    row_ids = jnp.arange(MAXSEC, dtype=jnp.int32)
    sector_ids = jnp.arange(SECTORS, dtype=jnp.int32)
    keep_first = (row_ids[None, :] < sector_sizes[0][:, None]).astype(jnp.float32)
    current = (env_in.astype(jnp.float32) * keep_first[None, None, :, :, None]).astype(jnp.bfloat16)
    outputs = []
    for site_index in range(SITES):
        keep_in = (row_ids[None, :] < sector_sizes[site_index][:, None]).astype(jnp.float32)
        out_sizes = sector_sizes[site_index + 1][targets[site_index]]
        keep_out = (row_ids[None, None, :] < out_sizes[:, :, None]).astype(jnp.float32)
        tensor = site_tensor[site_index].astype(jnp.float32) * keep_in[:, :, None, None] * keep_out[:, None, :, :]
        bra_block = bra_tensor[site_index].astype(jnp.float32)
        weights = mixing[site_index].astype(jnp.float32)
        onehot = (targets[site_index][:, :, None] == sector_ids[None, None, :]).astype(jnp.float32)

        def advance(env_block):
            mixed_env = jnp.einsum('sdc,camk->dsamk', weights, env_block.astype(jnp.float32), precision=lax.Precision.HIGHEST).astype(jnp.bfloat16)
            left_part = jnp.einsum('aiso,dsaik->dsaok', tensor, mixed_env.astype(jnp.float32)).astype(jnp.bfloat16)
            partial_value = jnp.einsum('dsaok,aksl->dsaol', left_part.astype(jnp.float32), bra_block).astype(jnp.bfloat16)
            return jnp.einsum('asj,dsaol->djol', onehot, partial_value.astype(jnp.float32)).astype(jnp.bfloat16)

        current = lax.map(advance, current)
        outputs.append(current)
    summed = jnp.sum(current.astype(jnp.float32), axis=0).astype(jnp.bfloat16)
    return jnp.stack(outputs), summed
```

```python
import functools

import jax
import jax.numpy as jnp
from jax import lax
from jax.experimental import pallas as pl
from jax.experimental.pallas import tpu as pltpu
from jax.sharding import PartitionSpec as P

GROUP = 2
REACH = 3


def sector_steps(sectors):
    if sectors <= 2 * REACH + 1:
        return list(range(sectors))
    return list(range(REACH + 1)) + [sectors - r for r in range(REACH, 0, -1)]


def kernel(
    sections, sectors, batches,
    env_ref, site_ref, bra_ref, mixing_ref, sizes_ref, targets_ref,
    out_ref, total_ref,
    gathered, outgoing, received, weights, acc, last, parts,
    ag_send, ag_recv, rt_send, rt_recv, tot_send, tot_recv, out_sem,
):
    sites, states, rows, full = site_ref.shape
    comps = env_ref.shape[0]
    width = env_ref.shape[2]
    steps = sector_steps(sectors)
    chunks = comps // GROUP
    share = comps // batches
    me_z = lax.axis_index("section")
    me_a = lax.axis_index("sector")
    me_b = lax.axis_index("comp")
    wrap = lambda value, count: lax.rem(value + count, count)
    forward = sections == 4

    barrier = pltpu.get_barrier_semaphore()
    greeted = 0
    for r in range(1, sections):
        pl.semaphore_signal(barrier, inc=1, device_id={"section": wrap(me_z + r, sections)},
                            device_id_type=pl.DeviceIdType.MESH)
        greeted += 1
    for r in steps[1:]:
        pl.semaphore_signal(barrier, inc=1, device_id={"sector": wrap(me_a + r, sectors)},
                            device_id_type=pl.DeviceIdType.MESH)
        greeted += 1
    for r in range(1, batches):
        pl.semaphore_signal(barrier, inc=1, device_id={"comp": wrap(me_b + r, batches)},
                            device_id_type=pl.DeviceIdType.MESH)
        greeted += 1
    pl.semaphore_wait(barrier, greeted)

    def gather_copy(t, q, owner, target, send_slot):
        block = gathered.at[t, owner, pl.ds(q * GROUP, GROUP)]
        return pltpu.make_async_remote_copy(
            src_ref=block, dst_ref=block,
            send_sem=ag_send.at[t, q, send_slot], recv_sem=ag_recv.at[t, q, owner],
            device_id={"section": target}, device_id_type=pl.DeviceIdType.MESH)

    def direct(z):
        near = jnp.abs(me_z - z) < sections - 1 if forward else True
        return jnp.logical_and(me_z != z, near)

    def gather_start(t, q):
        for z in range(sections):
            @pl.when(direct(z))
            def _():
                gather_copy(t, q, me_z, z, z).start()

    def gather_finish(t, q):
        if forward:
            for via, origin, end in ((1, 3, 0), (2, 0, 3)):
                @pl.when(me_z == via)
                def _():
                    gather_copy(t, q, origin, end, sections).wait_recv()
                    gather_copy(t, q, origin, end, sections).start()
        for z in range(sections):
            here = me_z != z
            if forward and z in (0, 3):
                here = jnp.logical_and(here, me_z != (2 if z == 0 else 1))

            @pl.when(here)
            def _():
                gather_copy(t, q, z, z, z).wait_recv()

    def gather_drain(t, q):
        for z in range(sections):
            @pl.when(direct(z))
            def _():
                gather_copy(t, q, me_z, z, z).wait_send()
        if forward:
            for via, origin, end in ((1, 3, 0), (2, 0, 3)):
                @pl.when(me_z == via)
                def _():
                    gather_copy(t, q, origin, end, sections).wait_send()

    def route_copy(t, q, j):
        chunk = pl.ds(q * GROUP, GROUP)
        return pltpu.make_async_remote_copy(
            src_ref=outgoing.at[t, j - 1, chunk], dst_ref=received.at[t, j, chunk],
            send_sem=rt_send.at[t, q, j], recv_sem=rt_recv.at[t, q, j],
            device_id={"sector": wrap(me_a + steps[j], sectors)},
            device_id_type=pl.DeviceIdType.MESH)

    def state_towards(t, source, target):
        state = jnp.int32(0)
        found = jnp.int32(0)
        for s in range(states):
            hit = targets_ref[t, source, s] == target
            state = jnp.where(hit, s, state)
            found = jnp.where(hit, 1, found)
        return state, found

    gathered[0, me_z] = env_ref[...]
    for q in range(chunks):
        gather_start(0, q)

    for t in range(sites):
        for j, step in enumerate(steps):
            target = wrap(me_a + step, sectors)
            state, found = state_towards(t, me_a, target)
            size_in = sizes_ref[t, me_a]
            size_out = sizes_ref[t + 1, target] * found
            o_ids = me_z * rows + lax.broadcasted_iota(jnp.int32, (rows, full), 0)
            i_ids = lax.broadcasted_iota(jnp.int32, (rows, full), 1)
            keep = jnp.logical_and(i_ids < size_in, o_ids < size_out)
            block = site_ref[t, state].astype(jnp.float32)
            weights[t, pl.ds(j * rows, rows)] = jnp.where(keep, block, 0.0).astype(jnp.bfloat16)

    def produce(t, q):
        columns = []
        for g in range(GROUP):
            column = gathered[t, :, q * GROUP + g].reshape(full, width)
            if t == 0:
                ids = lax.broadcasted_iota(jnp.int32, (full, width), 0)
                column = jnp.where(ids < sizes_ref[0, me_a], column.astype(jnp.float32), 0.0)
                column = column.astype(jnp.bfloat16)
            columns.append(column)
        left = jnp.dot(weights[t], jnp.concatenate(columns, axis=1),
                       preferred_element_type=jnp.float32).astype(jnp.bfloat16)
        for j in list(range(1, len(steps))) + [0]:
            state, _ = state_towards(t, me_a, wrap(me_a + steps[j], sectors))
            stacked = jnp.concatenate(
                [left[j * rows:(j + 1) * rows, g * width:(g + 1) * width] for g in range(GROUP)],
                axis=0)
            value = jnp.dot(stacked, bra_ref[t, state], preferred_element_type=jnp.float32)
            value = value.astype(jnp.bfloat16).reshape(GROUP, rows, width)
            if j:
                outgoing[t, j - 1, pl.ds(q * GROUP, GROUP)] = value
                route_copy(t, q, j).start()
            else:
                received[t, 0, pl.ds(q * GROUP, GROUP)] = value

    def route_finish(t, q):
        for j in range(1, len(steps)):
            route_copy(t, q, j).wait_recv()

    def combine(t, q, first, count, store):
        states_in = [state_towards(t, wrap(me_a - r, sectors), me_a)[0] for r in steps]
        factors = [[[mixing_ref[t, states_in[j], first + i, q * GROUP + g]
                     for g in range(GROUP)] for j in range(len(steps))] for i in range(count)]

        def tile(r, carry):
            where = pl.ds(pl.multiple_of(r * 32, 32), 32)
            terms = [[received[t, j, q * GROUP + g, where].astype(jnp.float32)
                      for g in range(GROUP)] for j in range(len(steps))]
            for i in range(count):
                value = None if q == 0 else acc[first + i, where]
                for j in range(len(steps)):
                    for g in range(GROUP):
                        term = terms[j][g] * factors[i][j][g]
                        value = term if value is None else value + term
                store(first + i, where, value)
            return carry

        lax.fori_loop(0, rows // 32, tile, 0)

    def keep_sum(d, where, value):
        acc[d, where] = value

    def total_copy(r):
        peer = wrap(me_b + r, batches)
        return pltpu.make_async_remote_copy(
            src_ref=last.at[pl.ds(peer * share, share)], dst_ref=parts.at[r - 1],
            send_sem=tot_send.at[r - 1], recv_sem=tot_recv.at[r - 1],
            device_id={"comp": peer}, device_id_type=pl.DeviceIdType.MESH)

    out_copies = []
    for t in range(sites):
        for q in range(chunks):
            gather_finish(t, q)
            produce(t, q)
            if q:
                route_finish(t, q - 1)
                for first in range(0, comps, 4):
                    combine(t, q - 1, first, 4, keep_sum)
        q = chunks - 1
        route_finish(t, q)
        if t + 1 < sites:
            def keep_next(d, where, value, t=t):
                gathered[t + 1, me_z, d, where] = value.astype(jnp.bfloat16)

            for nxt in range(chunks):
                combine(t, q, nxt * GROUP, GROUP, keep_next)
                gather_start(t + 1, nxt)
            copy = pltpu.make_async_copy(gathered.at[t + 1, me_z], out_ref.at[t, 0, :, 0], out_sem.at[t])
        else:
            def keep_last(d, where, value):
                last[d, where] = value.astype(jnp.bfloat16)

            for r in list(range(1, batches)) + [0]:
                combine(t, q, wrap(me_b + r, batches) * share, share, keep_last)
                if r:
                    total_copy(r).start()
            copy = pltpu.make_async_copy(last, out_ref.at[t, 0, :, 0], out_sem.at[t])
        copy.start()
        out_copies.append(copy)

    for t in range(sites):
        for q in range(chunks):
            gather_drain(t, q)
            for j in range(1, len(steps)):
                route_copy(t, q, j).wait_send()
    summed = last[pl.ds(me_b * share, share)].astype(jnp.float32)
    for r in range(1, batches):
        total_copy(r).wait_recv()
        summed = summed + parts[r - 1].astype(jnp.float32)
    total_ref[:, 0] = summed.astype(jnp.bfloat16)
    for r in range(1, batches):
        total_copy(r).wait_send()
    for copy in out_copies:
        copy.wait()


def local(sections, sectors, batches, env_in, site_tensor, bra_tensor, mixing, sector_sizes, targets):
    env = env_in[0, :, 0]
    site = jnp.transpose(site_tensor[:, 0], (0, 2, 3, 1))
    bra = jnp.transpose(bra_tensor[:, 0], (0, 2, 1, 3))
    sites, states, rows, full = site.shape
    comps, _, width = env.shape
    slots = len(sector_steps(sectors))
    chunks = comps // GROUP
    share = comps // batches
    vmem = pl.BlockSpec(memory_space=pltpu.VMEM)
    smem = pl.BlockSpec(memory_space=pltpu.SMEM)
    dma = pltpu.SemaphoreType.DMA
    return pl.pallas_call(
        functools.partial(kernel, sections, sectors, batches),
        out_shape=(
            jax.ShapeDtypeStruct((sites, 1, comps, 1, rows, width), jnp.bfloat16),
            jax.ShapeDtypeStruct((share, 1, rows, width), jnp.bfloat16),
        ),
        in_specs=[vmem, vmem, vmem, smem, smem, smem],
        out_specs=(pl.BlockSpec(memory_space=pl.ANY), vmem),
        scratch_shapes=[
            pltpu.VMEM((sites, sections, comps, rows, width), jnp.bfloat16),
            pltpu.VMEM((sites, max(slots - 1, 1), comps, rows, width), jnp.bfloat16),
            pltpu.VMEM((sites, slots, comps, rows, width), jnp.bfloat16),
            pltpu.VMEM((sites, slots * rows, full), jnp.bfloat16),
            pltpu.VMEM((comps, rows, width), jnp.float32),
            pltpu.VMEM((comps, rows, width), jnp.bfloat16),
            pltpu.VMEM((max(batches - 1, 1), share, rows, width), jnp.bfloat16),
            dma((sites, chunks, sections + 1)),
            dma((sites, chunks, sections)),
            dma((sites, chunks, slots)),
            dma((sites, chunks, slots)),
            dma((max(batches - 1, 1),)),
            dma((max(batches - 1, 1),)),
            dma((sites,)),
        ],
        compiler_params=pltpu.CompilerParams(
            collective_id=0, has_side_effects=True, vmem_limit_bytes=40 * 1024 * 1024),
    )(env, site, bra, mixing, sector_sizes, targets)


def solution(mesh):
    in_specs = (
        P("comp", None, "sector", "section", None),
        P(None, "sector", None, None, "section"),
        P(None, "sector", None, None, None),
        P(),
        P(),
        P(),
    )
    out_specs = (
        P(None, "comp", None, "sector", "section", None),
        P("comp", "sector", "section", None),
    )
    body = functools.partial(local, mesh.shape["section"], mesh.shape["sector"], mesh.shape["comp"])
    return jax.shard_map(body, mesh=mesh, in_specs=in_specs, out_specs=out_specs, check_vma=False)
```

```python
import functools

import jax
import jax.numpy as jnp
from jax import lax
from jax.experimental import pallas as pl
from jax.experimental.pallas import tpu as pltpu
from jax.sharding import PartitionSpec as P

LEAD = 1
SIZES = (2, 2, 2, 2)
WINDOW = 9
REACH = 3


def sector_steps(sectors):
    if sectors <= 2 * REACH + 1:
        return list(range(sectors))
    return list(range(REACH + 1)) + [sectors - r for r in range(REACH, 0, -1)]


def kernel(
    sections, sectors, batches,
    env_ref, site_ref, bra_ref, mixing_ref, sizes_ref, targets_ref,
    out_ref, total_ref,
    gathered, outgoing, received, weights, acc, last, parts,
    ag_send, ag_recv, rt_send, rt_recv, tot_send, tot_recv, out_sem,
):
    sites, states, rows, full = site_ref.shape
    comps = env_ref.shape[0]
    width = env_ref.shape[2]
    steps = sector_steps(sectors)
    chunks = len(SIZES)
    starts = [sum(SIZES[:q]) for q in range(chunks)]
    share = comps // batches
    me_z = lax.axis_index("section")
    me_a = lax.axis_index("sector")
    me_b = lax.axis_index("comp")
    wrap = lambda value, count: lax.rem(value + count, count)
    forward = sections == 4

    barrier = pltpu.get_barrier_semaphore()
    greeted = 0
    for r in range(1, sections):
        pl.semaphore_signal(barrier, inc=1, device_id={"section": wrap(me_z + r, sections)},
                            device_id_type=pl.DeviceIdType.MESH)
        greeted += 1
    for r in steps[1:]:
        pl.semaphore_signal(barrier, inc=1, device_id={"sector": wrap(me_a + r, sectors)},
                            device_id_type=pl.DeviceIdType.MESH)
        greeted += 1
    for r in range(1, batches):
        pl.semaphore_signal(barrier, inc=1, device_id={"comp": wrap(me_b + r, batches)},
                            device_id_type=pl.DeviceIdType.MESH)
        greeted += 1
    pl.semaphore_wait(barrier, greeted)

    def gather_copy(t, q, owner, target, send_slot):
        block = gathered.at[t, owner, pl.ds(starts[q], SIZES[q])]
        return pltpu.make_async_remote_copy(
            src_ref=block, dst_ref=block,
            send_sem=ag_send.at[t, q, send_slot], recv_sem=ag_recv.at[t, q, owner],
            device_id={"section": target}, device_id_type=pl.DeviceIdType.MESH)

    def direct(z):
        near = jnp.abs(me_z - z) < sections - 1 if forward else True
        return jnp.logical_and(me_z != z, near)

    inner = jnp.logical_or(me_z == 1, me_z == 2)

    def gather_start(t, q, late=False):
        for z in range(sections):
            chosen = direct(z)
            if forward and late:
                chosen = jnp.logical_and(chosen, inner)
            elif forward and q >= WINDOW:
                chosen = jnp.logical_and(chosen, jnp.logical_not(inner))

            @pl.when(chosen)
            def _():
                gather_copy(t, q, me_z, z, z).start()

    def gather_forward(t, q):
        for via, origin, end in ((1, 3, 0), (2, 0, 3)):
            @pl.when(me_z == via)
            def _():
                gather_copy(t, q, origin, end, sections).wait_recv()
                gather_copy(t, q, origin, end, sections).start()
        if q + WINDOW < chunks:
            gather_start(t, q + WINDOW, late=True)

    def gather_finish(t, q):
        if forward:
            for ahead in range(q + LEAD if q else 0, min(q + LEAD + 1, chunks)):
                gather_forward(t, ahead)
        for z in range(sections):
            here = me_z != z
            if forward and z in (0, 3):
                here = jnp.logical_and(here, me_z != (2 if z == 0 else 1))

            @pl.when(here)
            def _():
                gather_copy(t, q, z, z, z).wait_recv()

    def gather_drain(t, q):
        for z in range(sections):
            @pl.when(direct(z))
            def _():
                gather_copy(t, q, me_z, z, z).wait_send()
        if forward:
            for via, origin, end in ((1, 3, 0), (2, 0, 3)):
                @pl.when(me_z == via)
                def _():
                    gather_copy(t, q, origin, end, sections).wait_send()

    def route_copy(t, q, j):
        chunk = pl.ds(starts[q], SIZES[q])
        return pltpu.make_async_remote_copy(
            src_ref=outgoing.at[t, j - 1, chunk], dst_ref=received.at[t, j, chunk],
            send_sem=rt_send.at[t, q, j], recv_sem=rt_recv.at[t, q, j],
            device_id={"sector": wrap(me_a + steps[j], sectors)},
            device_id_type=pl.DeviceIdType.MESH)

    def state_towards(t, source, target):
        state = jnp.int32(0)
        found = jnp.int32(0)
        for s in range(states):
            hit = targets_ref[t, source, s] == target
            state = jnp.where(hit, s, state)
            found = jnp.where(hit, 1, found)
        return state, found

    gathered[0, me_z] = env_ref[...]
    for q in range(chunks):
        gather_start(0, q)

    for t in range(sites):
        for j, step in enumerate(steps):
            target = wrap(me_a + step, sectors)
            state, found = state_towards(t, me_a, target)
            size_in = sizes_ref[t, me_a]
            size_out = sizes_ref[t + 1, target] * found
            o_ids = me_z * rows + lax.broadcasted_iota(jnp.int32, (rows, full), 0)
            i_ids = lax.broadcasted_iota(jnp.int32, (rows, full), 1)
            keep = jnp.logical_and(i_ids < size_in, o_ids < size_out)
            block = site_ref[t, state].astype(jnp.float32)
            weights[t, pl.ds(j * rows, rows)] = jnp.where(keep, block, 0.0).astype(jnp.bfloat16)

    def produce(t, q):
        columns = []
        for g in range(SIZES[q]):
            column = gathered[t, :, starts[q] + g].reshape(full, width)
            if t == 0:
                ids = lax.broadcasted_iota(jnp.int32, (full, width), 0)
                column = jnp.where(ids < sizes_ref[0, me_a], column.astype(jnp.float32), 0.0)
                column = column.astype(jnp.bfloat16)
            columns.append(column)
        left = jnp.dot(weights[t], jnp.concatenate(columns, axis=1),
                       preferred_element_type=jnp.float32).astype(jnp.bfloat16)
        for j in list(range(1, len(steps))) + [0]:
            state, _ = state_towards(t, me_a, wrap(me_a + steps[j], sectors))
            stacked = jnp.concatenate(
                [left[j * rows:(j + 1) * rows, g * width:(g + 1) * width] for g in range(SIZES[q])],
                axis=0)
            value = jnp.dot(stacked, bra_ref[t, state], preferred_element_type=jnp.float32)
            value = value.astype(jnp.bfloat16).reshape(SIZES[q], rows, width)
            if j:
                outgoing[t, j - 1, pl.ds(starts[q], SIZES[q])] = value
                route_copy(t, q, j).start()
            else:
                received[t, 0, pl.ds(starts[q], SIZES[q])] = value

    def route_finish(t, q):
        for j in range(1, len(steps)):
            route_copy(t, q, j).wait_recv()

    def combine(t, q, first, count, store):
        states_in = [state_towards(t, wrap(me_a - r, sectors), me_a)[0] for r in steps]
        factors = [[[mixing_ref[t, states_in[j], first + i, starts[q] + g]
                     for g in range(SIZES[q])] for j in range(len(steps))] for i in range(count)]

        def tile(r, carry):
            where = pl.ds(pl.multiple_of(r * 32, 32), 32)
            terms = [[received[t, j, starts[q] + g, where].astype(jnp.float32)
                      for g in range(SIZES[q])] for j in range(len(steps))]
            for i in range(count):
                value = None if q == 0 else acc[first + i, where]
                for j in range(len(steps)):
                    for g in range(SIZES[q]):
                        term = terms[j][g] * factors[i][j][g]
                        value = term if value is None else value + term
                store(first + i, where, value)
            return carry

        lax.fori_loop(0, rows // 32, tile, 0)

    def keep_sum(d, where, value):
        acc[d, where] = value

    def total_copy(r):
        peer = wrap(me_b + r, batches)
        return pltpu.make_async_remote_copy(
            src_ref=last.at[pl.ds(peer * share, share)], dst_ref=parts.at[r - 1],
            send_sem=tot_send.at[r - 1], recv_sem=tot_recv.at[r - 1],
            device_id={"comp": peer}, device_id_type=pl.DeviceIdType.MESH)

    out_copies = []
    for t in range(sites):
        for q in range(chunks):
            gather_finish(t, q)
            produce(t, q)
            if q:
                route_finish(t, q - 1)
                for first in range(0, comps, 4):
                    combine(t, q - 1, first, 4, keep_sum)
        q = chunks - 1
        route_finish(t, q)
        if t + 1 < sites:
            def keep_next(d, where, value, t=t):
                gathered[t + 1, me_z, d, where] = value.astype(jnp.bfloat16)

            for nxt in range(chunks):
                combine(t, q, starts[nxt], SIZES[nxt], keep_next)
                gather_start(t + 1, nxt)
            copy = pltpu.make_async_copy(gathered.at[t + 1, me_z], out_ref.at[t, 0, :, 0], out_sem.at[t])
        else:
            def keep_last(d, where, value):
                last[d, where] = value.astype(jnp.bfloat16)

            for r in list(range(1, batches)) + [0]:
                combine(t, q, wrap(me_b + r, batches) * share, share, keep_last)
                if r:
                    total_copy(r).start()
            copy = pltpu.make_async_copy(last, out_ref.at[t, 0, :, 0], out_sem.at[t])
        copy.start()
        out_copies.append(copy)

    for t in range(sites):
        for q in range(chunks):
            gather_drain(t, q)
            for j in range(1, len(steps)):
                route_copy(t, q, j).wait_send()
    summed = last[pl.ds(me_b * share, share)].astype(jnp.float32)
    for r in range(1, batches):
        total_copy(r).wait_recv()
        summed = summed + parts[r - 1].astype(jnp.float32)
    total_ref[:, 0] = summed.astype(jnp.bfloat16)
    for r in range(1, batches):
        total_copy(r).wait_send()
    for copy in out_copies:
        copy.wait()


def local(sections, sectors, batches, env_in, site_tensor, bra_tensor, mixing, sector_sizes, targets):
    env = env_in[0, :, 0]
    site = jnp.transpose(site_tensor[:, 0], (0, 2, 3, 1))
    bra = jnp.transpose(bra_tensor[:, 0], (0, 2, 1, 3))
    sites, states, rows, full = site.shape
    comps, _, width = env.shape
    slots = len(sector_steps(sectors))
    chunks = len(SIZES)
    share = comps // batches
    vmem = pl.BlockSpec(memory_space=pltpu.VMEM)
    smem = pl.BlockSpec(memory_space=pltpu.SMEM)
    dma = pltpu.SemaphoreType.DMA
    return pl.pallas_call(
        functools.partial(kernel, sections, sectors, batches),
        out_shape=(
            jax.ShapeDtypeStruct((sites, 1, comps, 1, rows, width), jnp.bfloat16),
            jax.ShapeDtypeStruct((share, 1, rows, width), jnp.bfloat16),
        ),
        in_specs=[vmem, vmem, vmem, smem, smem, smem],
        out_specs=(pl.BlockSpec(memory_space=pl.ANY), vmem),
        scratch_shapes=[
            pltpu.VMEM((sites, sections, comps, rows, width), jnp.bfloat16),
            pltpu.VMEM((sites, max(slots - 1, 1), comps, rows, width), jnp.bfloat16),
            pltpu.VMEM((sites, slots, comps, rows, width), jnp.bfloat16),
            pltpu.VMEM((sites, slots * rows, full), jnp.bfloat16),
            pltpu.VMEM((comps, rows, width), jnp.float32),
            pltpu.VMEM((comps, rows, width), jnp.bfloat16),
            pltpu.VMEM((max(batches - 1, 1), share, rows, width), jnp.bfloat16),
            dma((sites, chunks, sections + 1)),
            dma((sites, chunks, sections)),
            dma((sites, chunks, slots)),
            dma((sites, chunks, slots)),
            dma((max(batches - 1, 1),)),
            dma((max(batches - 1, 1),)),
            dma((sites,)),
        ],
        compiler_params=pltpu.CompilerParams(
            collective_id=0, has_side_effects=True, vmem_limit_bytes=40 * 1024 * 1024),
    )(env, site, bra, mixing, sector_sizes, targets)


def solution(mesh):
    in_specs = (
        P("comp", None, "sector", "section", None),
        P(None, "sector", None, None, "section"),
        P(None, "sector", None, None, None),
        P(),
        P(),
        P(),
    )
    out_specs = (
        P(None, "comp", None, "sector", "section", None),
        P("comp", "sector", "section", None),
    )
    body = functools.partial(local, mesh.shape["section"], mesh.shape["sector"], mesh.shape["comp"])
    return jax.shard_map(body, mesh=mesh, in_specs=in_specs, out_specs=out_specs, check_vma=False)
```
